512 devices in a mesh: row: 16 (over x, y_hi, core), col: 32 (over y_lo, z).
Axes of the slice: x: 4, y: 4 (y_hi: 2, y_lo: 2; y = y_hi * 2 + y_lo), z: 16, core: 2. Of those that a mesh axis runs over, the one named last changes fastest.
Arguments:
- hidden_in: bfloat16 [2048, 4096], P('row', 'col'), may hold values from -16 to 16
- norm_gain: bfloat16 [4096], P('col'), may hold values from 0.3 to 3
- w_query: bfloat16 [4096, 4096], P('row', 'col'), may hold values from -0.09375 to 0.09375
- w_key: bfloat16 [4096, 4096], P('row', 'col'), may hold values from -0.09375 to 0.09375
- w_value: bfloat16 [4096, 4096], P('row', 'col'), may hold values from -0.09375 to 0.09375
- w_out: bfloat16 [4096, 4096], P('row', 'col'), may hold values from -0.09375 to 0.09375
- packet_ids: int32 [2048], replicated, may hold values from 0 to 63, never falling along the last dimension, each value on 1 to 96 neighbouring positions
- grad_out: bfloat16 [2048, 4096], P('row', 'col'), may hold values from -6 to 6
Outputs:
- mixed: bfloat16 [2048, 4096], P('row', 'col')
- grad_x: float32 [2048, 4096], P('row', 'col')
- grad_gain: float32 [4096], P('col')
- grad_w_query: float32 [4096, 4096], P('row', 'col')
- grad_w_key: float32 [4096, 4096], P('row', 'col')
- grad_w_value: float32 [4096, 4096], P('row', 'col')
- grad_w_out: float32 [4096, 4096], P('row', 'col')
The draws below stay inside these ranges and needn't reach their ends.
Inputs may be any that keep to these rules, and one draw needn't show every extreme that they name: `packet_ids`: packet ids never fall along the tokens; each of the 64 packets holds 1 to 96 tokens, at least one exactly 96.
All inputs are finite; a program needn't handle non-finite values.
Results may differ from the reference program's by a relative error of at most 0.035.
Values may be sent and summed in bfloat16 or wider, within the bound.
No kernel may reach another device: no remote copies, remote signals or barrier semaphores. Data moves between devices by JAX's collectives and lax.ppermute only.
A program may use at most 64 MiB of HBM per device.

```python
import math
import jax
import jax.numpy as jnp
import numpy as np
from jax import lax

D = 4096
H = 32
HD = 128
TOKENS = 2048
PACKETS = 64
PACKET_MOST = 96
N_COL = 32


def draw_hidden_in(key, part):
    key = jax.random.fold_in(key, 11)
    key_base, key_factor = jax.random.split(key)
    position = jnp.arange(D, dtype=jnp.float32) / D
    base = jnp.clip(jax.random.normal(key_base, (TOKENS, D), jnp.float32), -4.0, 4.0)
    column = 0.3 * jnp.power(10.0, position)
    factor = jax.random.uniform(key_factor, (D,), jnp.float32, 0.8, 1.25)
    return (base * (column * factor)[None, :]).astype(jnp.bfloat16)


def draw_norm_gain(key, part):
    key = jax.random.fold_in(key, 23)
    position = jnp.arange(D, dtype=jnp.float32) / D
    factor = jnp.exp(jax.random.uniform(key, (D,), jnp.float32, -0.15, 0.15))
    gain = 0.5 * jnp.power(4.0, position) * factor
    return gain.astype(jnp.bfloat16)


def steps_of(stream_key, dims, pieces, least, high):
    def one(axis_at, parts):
        steps = jax.random.uniform(jax.random.fold_in(jax.random.fold_in(stream_key, 6), axis_at), (parts,), jnp.float32, least / len(pieces), high / len(pieces))
        return jnp.repeat(jnp.exp(steps), dims[axis_at] // parts).reshape((-1,) + (1,) * (len(dims) - axis_at - 1))

    level = one(*pieces[0])
    for cut in pieces[1:]:
        level = level * one(*cut)
    return level


def split_up(amount, total, most, slope):
    loads = [(1 << 20) // math.isqrt(grade ** slope) + 1 for grade in range(2, amount + 1)]
    spare, holding = total - most - (amount - 1), [1] * (amount - 1)
    while spare > 0:
        movable = [i for i in range(amount - 1) if holding[i] < most]
        mass, budget = sum([loads[i] for i in movable]), spare
        for i in movable:
            more = min(most - holding[i], max(1, budget * loads[i] // mass), spare)
            holding[i] = holding[i] + more
            spare = spare - more
    return np.array([most] + holding)


def uneven(own_key, amount, total, bound, skew):
    if amount == 2:
        one = jax.random.randint(own_key, (), max(1, total - bound), min(bound, total - 1) + 1)
        return jnp.stack([one, total - one])
    lengths = jnp.asarray(split_up(amount, total, bound, skew), jnp.int32)
    couples = (amount - 1) // 2
    source_of, sink = lengths[1:1 + 2 * couples:2], lengths[2:2 + 2 * couples:2]
    room = jnp.minimum(source_of - 1, bound - sink)
    shifted = jax.random.randint(jax.random.fold_in(own_key, 1), (couples,), 0, 1 << 20) % (room + 1)
    lengths = lengths.at[1:1 + 2 * couples:2].set(source_of - shifted).at[2:2 + 2 * couples:2].set(sink + shifted)
    return lengths[jax.random.permutation(jax.random.fold_in(own_key, 2), amount)]


def scatter_about(key, dims, width, most, cuts=(), kind=jnp.bfloat16):
    values = jax.random.normal(key, dims, jnp.float32) * width
    if len(cuts) > 0:
        values = steps_of(key, dims, cuts, -0.22, 0.18) * values
    return jnp.clip(values, min=-most, max=most).astype(kind)


def setup_inputs(seed: int = 0) -> dict:
    keys = jax.random.split(jax.random.key(seed), 9)
    hidden_in = draw_hidden_in(jax.random.fold_in(keys[8], 71), 0)
    norm_gain = draw_norm_gain(jax.random.fold_in(keys[8], 71), 0)
    w_query = scatter_about(keys[2], (D, D), D ** -0.5, 0.09375, ((0, 16), (1, 32)))
    w_key = scatter_about(keys[3], (D, D), D ** -0.5, 0.09375, ((0, 16), (1, 32)))
    w_value = scatter_about(keys[4], (D, D), D ** -0.5, 0.09375, ((0, 16), (1, 32)))
    w_out = scatter_about(keys[5], (D, D), D ** -0.5, 0.09375, ((0, 16), (1, 32)))
    packet_ids = jnp.searchsorted(jnp.cumsum(uneven(keys[6], PACKETS, TOKENS, PACKET_MOST, 1)), jnp.arange(TOKENS), side="right").astype(jnp.int32)
    grad_out = scatter_about(keys[7], (TOKENS, D), 1.0, 6.0, ((0, 16), (1, 32)))
    return dict(hidden_in=hidden_in, norm_gain=norm_gain, w_query=w_query, w_key=w_key, w_value=w_value, w_out=w_out, packet_ids=packet_ids, grad_out=grad_out)


norm_eps = 1e-05

def soft_probs(query_h, key_h, allowed):
    scores = jnp.dot(query_h, key_h.T, preferred_element_type=jnp.float32) * HD ** (-0.5)
    scores = jnp.where(allowed, scores, -1e+30)
    row_max = lax.optimization_barrier(jnp.max(scores, axis=1, keepdims=True))
    exponent = jnp.where(allowed, jnp.exp(scores - row_max), 0.0)
    return exponent / lax.optimization_barrier(jnp.sum(exponent, axis=1, keepdims=True))

def reference(hidden_in, norm_gain, w_query, w_key, w_value, w_out, packet_ids, grad_out):
    tok_total = hidden_in.shape[0]
    x_float = hidden_in.astype(jnp.float32)
    recip = lax.rsqrt(lax.optimization_barrier(jnp.mean(x_float * x_float, axis=1)) + norm_eps)
    gain_float = norm_gain.astype(jnp.float32)
    normed = (x_float * recip[:, None] * gain_float).astype(jnp.bfloat16)
    query = jnp.dot(normed, w_query, preferred_element_type=jnp.float32).astype(jnp.bfloat16)
    key = jnp.dot(normed, w_key, preferred_element_type=jnp.float32).astype(jnp.bfloat16)
    value = jnp.dot(normed, w_value, preferred_element_type=jnp.float32).astype(jnp.bfloat16)
    allowed = packet_ids[None, :] <= packet_ids[:, None]

    def split_heads(array):
        return array.reshape(tok_total, H, HD).transpose(1, 0, 2)

    def join_heads(array):
        return array.transpose(1, 0, 2).reshape(tok_total, D)

    def forward_head(items):
        query_h, key_h, value_h = items
        probs = soft_probs(query_h, key_h, allowed)
        return jnp.dot(probs.astype(jnp.bfloat16), value_h, preferred_element_type=jnp.float32).astype(jnp.bfloat16)
    attended = join_heads(lax.map(forward_head, (split_heads(query), split_heads(key), split_heads(value))))
    mixed = (x_float + jnp.dot(attended, w_out, preferred_element_type=jnp.float32)).astype(jnp.bfloat16)
    group_w = D // N_COL

    def head_group(index, total):
        start = (index * group_w).astype(jnp.int32)
        grad_cols = lax.dynamic_slice_in_dim(grad_out, start, group_w, 1)
        weight_cols = lax.dynamic_slice_in_dim(w_out, start, group_w, 1)
        part = jnp.dot(grad_cols, weight_cols.T, preferred_element_type=jnp.float32)
        return total + lax.optimization_barrier(part.astype(jnp.bfloat16)).astype(jnp.float32)
    grad_heads = lax.fori_loop(0, N_COL, head_group, jnp.zeros((tok_total, D), jnp.float32)).astype(jnp.bfloat16)
    grad_w_out = jnp.dot(attended.T, grad_out, preferred_element_type=jnp.float32)

    def backward_head(items):
        query_h, key_h, value_h, grad_h = items
        probs = soft_probs(query_h, key_h, allowed)
        probs_low = probs.astype(jnp.bfloat16)
        dprob = jnp.dot(grad_h, value_h.T, preferred_element_type=jnp.float32)
        row_delta = lax.optimization_barrier(jnp.sum(dprob * probs, axis=1, keepdims=True))
        dscore = (probs * (dprob - row_delta)).astype(jnp.bfloat16)
        grad_q = (jnp.dot(dscore, key_h, preferred_element_type=jnp.float32) * HD ** (-0.5)).astype(jnp.bfloat16)
        grad_k = (jnp.dot(dscore.T, query_h, preferred_element_type=jnp.float32) * HD ** (-0.5)).astype(jnp.bfloat16)
        grad_v = jnp.dot(probs_low.T, grad_h, preferred_element_type=jnp.float32).astype(jnp.bfloat16)
        return (grad_q, grad_k, grad_v)
    grad_qh, grad_kh, grad_vh = lax.map(backward_head, (split_heads(query), split_heads(key), split_heads(value), split_heads(grad_heads)))
    grad_query = join_heads(grad_qh)
    grad_key = join_heads(grad_kh)
    grad_value = join_heads(grad_vh)

    def input_group(index, total):
        start = (index * group_w).astype(jnp.int32)
        part = jnp.zeros((tok_total, D), jnp.float32)
        for grad_full, weight_full in ((grad_query, w_query), (grad_key, w_key), (grad_value, w_value)):
            grad_cols = lax.dynamic_slice_in_dim(grad_full, start, group_w, 1)
            weight_cols = lax.dynamic_slice_in_dim(weight_full, start, group_w, 1)
            part = part + jnp.dot(grad_cols, weight_cols.T, preferred_element_type=jnp.float32)
        return total + lax.optimization_barrier(part.astype(jnp.bfloat16)).astype(jnp.float32)
    grad_normed = lax.fori_loop(0, N_COL, input_group, jnp.zeros((tok_total, D), jnp.float32))
    grad_w_query = jnp.dot(normed.T, grad_query, preferred_element_type=jnp.float32)
    grad_w_key = jnp.dot(normed.T, grad_key, preferred_element_type=jnp.float32)
    grad_w_value = jnp.dot(normed.T, grad_value, preferred_element_type=jnp.float32)
    scaled = grad_normed * gain_float
    feat_dot = lax.optimization_barrier(jnp.sum(scaled * x_float, axis=1))
    grad_gain = lax.optimization_barrier(jnp.sum(grad_normed * x_float * recip[:, None], axis=0))
    grad_x = grad_out.astype(jnp.float32) + recip[:, None] * scaled - x_float * (recip * recip * recip * feat_dot / D)[:, None]
    return (mixed, grad_x, grad_gain, grad_w_query, grad_w_key, grad_w_value, grad_w_out)
```

```python
import jax
import jax.numpy as jnp
from jax import lax
from jax.experimental import pallas as pl
from jax.experimental.pallas import tpu as pltpu
from jax.sharding import PartitionSpec as P

D = 4096
HD = 128
TOK = 2048
BLOCK = 256
OVER = 128
SCALE = HD ** (-0.5)
MASKED = -1e30
norm_eps = 1e-05

F32 = jnp.float32
BF16 = jnp.bfloat16


def col_at(a, h, l):
    return a * 16 + 2 * h + l


FAR = [[col_at(a, h, l) for h in range(8)] for a in range(2) for l in range(2)]
NEAR = [[col_at(a, h, l) for a in range(2) for l in range(2)] for h in range(8)]
CHIPS = [[2 * k + core for k in range(8)] for core in range(2)]
CORE_SWAP = [(r, r ^ 1) for r in range(16)]
TURN = [(r * 32 + c, (c // 2) * 32 + 2 * r + c % 2) for r in range(16) for c in range(32)]
TURN_ODD = [(r * 32 + c, (c // 2) * 32 + 2 * r + 1 - c % 2) for r in range(16) for c in range(32)]


def mm(a, b):
    return jnp.dot(a, b, preferred_element_type=F32)


def mm_nt(a, b):
    return lax.dot_general(a, b, (((1,), (1,)), ((), ())), preferred_element_type=F32)


def mm_tn(a, b):
    return lax.dot_general(a, b, (((0,), (0,)), ((), ())), preferred_element_type=F32)


def spread(x, axis, groups):
    n = len(groups[0])
    wide = jnp.broadcast_to(x[None], (n,) + x.shape)
    return lax.all_to_all(wide, axis, 0, 0, tiled=True, axis_index_groups=groups)


def flip(x):
    return x.astype(F32).T.astype(BF16)


def project_kernel(core_ref, wide, own, other, heads, both, recip_out):
    core = core_ref[0]
    squares = jnp.zeros((128, 128), F32)
    for a in range(2):
        for l in range(2):
            for h in range(8):
                x = wide[a, l, h, 0:128, :].astype(F32)
                squares = squares + x * x
    recip = lax.rsqrt(jnp.sum(squares, axis=1, keepdims=True) / D + norm_eps)
    recip_out[...] = recip
    qkv = jnp.zeros((128, 3 * HD), F32)
    grad = jnp.zeros((128, HD), F32)
    for k in range(8):
        for src, flag in ((own, core), (other, 1 - core)):
            h = 2 * (k % 4) + flag
            normed, go = [], []
            for l in range(2):
                x = wide[k // 4, l, h, 0:128, :].astype(F32)
                gain = wide[k // 4, l, h, 256:272, :].astype(F32)[0:1, :]
                normed.append((x * recip * gain).astype(BF16))
                go.append(wide[k // 4, l, h, 128:256, :])
            normed = jnp.concatenate(normed, axis=1)
            go = jnp.concatenate(go, axis=1)
            both[2 * k + flag, :, 0:256] = normed
            both[2 * k + flag, :, 256:512] = go
            qkv = qkv + mm(normed, src[k, :, 0 : 3 * HD])
            grad = grad + mm(go, src[k, :, 3 * HD :])
    heads[:, 0 : 3 * HD] = qkv.astype(BF16)
    heads[:, 3 * HD :] = grad.astype(BF16)


def project(core, wide, own, other):
    vmem = pl.BlockSpec(memory_space=pltpu.VMEM)
    return pl.pallas_call(
        project_kernel,
        out_shape=(
            jax.ShapeDtypeStruct((128, 4 * HD), BF16),
            jax.ShapeDtypeStruct((16, 128, 512), BF16),
            jax.ShapeDtypeStruct((128, 1), F32),
        ),
        in_specs=[pl.BlockSpec(memory_space=pltpu.SMEM), vmem, vmem, vmem],
        out_specs=(vmem, vmem, vmem),
        compiler_params=pltpu.CompilerParams(vmem_limit_bytes=48 * 1024 * 1024),
        name="project",
    )(core[None], wide, own, other)


def dot_rows(dot):
    high = dot.astype(BF16)
    low = (dot - high.astype(F32)).astype(BF16)
    at = lax.broadcasted_iota(jnp.int32, (16, 128), 0)
    wide = jnp.where(at == 0, high.astype(F32), jnp.where(at == 1, low.astype(F32), 0.0))
    return wide.astype(BF16)


def parts_kernel(place, grads, att, wide, w_own, w_other, parts):
    core, row = place[0], place[1]
    here = pl.ds(pl.multiple_of(row * 128, 128), 128)
    grad, attended = grads[here, :], att[here, :]
    dots = jnp.zeros((128, 128), F32)
    for k in range(8):
        for src, flag in ((w_own, core), (w_other, 1 - core)):
            h = 2 * (k % 4) + flag
            back = mm_nt(grad, src[k, :, 0 : 3 * HD]).astype(BF16)
            mixed = mm_nt(attended, src[k, :, 3 * HD :]).astype(BF16)
            for l in range(2):
                cut = slice(l * 128, (l + 1) * 128)
                x = wide[k // 4, l, h, 0:128, :].astype(F32)
                gain = wide[k // 4, l, h, 256:272, :].astype(F32)[0:1, :]
                dots = dots + back[:, cut].astype(F32) * gain * x
                parts[2 * (k // 4) + l, h, 0:128, :] = back[:, cut]
                parts[2 * (k // 4) + l, h, 128:256, :] = mixed[:, cut]
    extra = dot_rows(jnp.sum(dots.T, axis=0, keepdims=True))
    for n in range(4):
        for h in range(8):
            parts[n, h, 256:272, :] = extra


def to_parts(core, row, grads, att, wide, w_own, w_other):
    vmem = pl.BlockSpec(memory_space=pltpu.VMEM)
    return pl.pallas_call(
        parts_kernel,
        out_shape=jax.ShapeDtypeStruct((4, 8, 272, 128), BF16),
        in_specs=[pl.BlockSpec(memory_space=pltpu.SMEM)] + [vmem] * 5,
        out_specs=vmem,
        compiler_params=pltpu.CompilerParams(vmem_limit_bytes=48 * 1024 * 1024),
        name="to_parts",
    )(jnp.stack([core, row]), grads, att, wide, w_own, w_other)


def merge_kernel(parts, out):
    for h in range(8):
        total = parts[0, h].astype(F32)
        for n in range(1, 4):
            total = total + parts[n, h].astype(F32)
        out[h, 0:256, :] = total[0:256].astype(BF16)
        out[h, 256:272, :] = dot_rows(total[256:257] + total[257:258])


def merge(parts):
    vmem = pl.BlockSpec(memory_space=pltpu.VMEM)
    return pl.pallas_call(
        merge_kernel,
        out_shape=jax.ShapeDtypeStruct((8, 272, 128), BF16),
        in_specs=[vmem],
        out_specs=vmem,
        compiler_params=pltpu.CompilerParams(vmem_limit_bytes=48 * 1024 * 1024),
        name="merge",
    )(parts)


def finish_kernel(parts, hidden, gain_in, recip_in, grad_out, mixed, grad_x, gain_part):
    total = parts[0].astype(F32)
    for n in range(1, 8):
        total = total + parts[n].astype(F32)
    grad_normed = total[0:128]
    dot = total[256:257] + total[257:258]
    dot = jnp.broadcast_to(dot, (128, 128)).T
    x = hidden[...].astype(F32)
    recip = recip_in[...]
    mixed[...] = (x + total[128:256]).astype(BF16)
    scaled = grad_normed * gain_in[...].astype(F32)
    grad_x[...] = grad_out[...].astype(F32) + recip * scaled - x * (recip * recip * recip * dot / D)
    part = jnp.sum(grad_normed * x * recip, axis=0, keepdims=True)
    for n in range(16):
        gain_part[n] = part


def finish(parts, hidden, gain, recip, grad_out):
    vmem = pl.BlockSpec(memory_space=pltpu.VMEM)
    return pl.pallas_call(
        finish_kernel,
        out_shape=(
            jax.ShapeDtypeStruct((128, 128), BF16),
            jax.ShapeDtypeStruct((128, 128), F32),
            jax.ShapeDtypeStruct((16, 1, 128), F32),
        ),
        in_specs=[vmem] * 5,
        out_specs=(vmem, vmem, vmem),
        name="finish",
    )(parts, hidden, gain[None, :], recip, grad_out)


def attention_kernel(
    core_ref, ids_row, ids_col, own, other, grads, att,
    q_s, k_s, v_s, g_s, q_t, k_t, v_t, g_t, s_s, e_s, dk_s, dv_s,
):
    core = core_ref[0]
    for k in range(8):
        for src, flag in ((own, core), (other, 1 - core)):
            at = pl.ds(pl.multiple_of((2 * k + flag) * 128, 128), 128)
            for n, (flat, turned) in enumerate(((q_s, q_t), (k_s, k_t), (v_s, v_t), (g_s, g_t))):
                piece = src[k, :, n * 128 : (n + 1) * 128]
                flat[at, :] = piece
                turned[:, at] = flip(piece)
    dk_s[...] = jnp.zeros_like(dk_s)
    dv_s[...] = jnp.zeros_like(dv_s)
    for i in range(TOK // BLOCK):
        base = i * BLOCK
        here = slice(base, base + BLOCK)
        tiles = [(j * BLOCK, BLOCK) for j in range(i + 1)]
        if base + BLOCK < TOK:
            tiles.append((base + BLOCK, OVER))
        query_t = q_t[:, here]
        top = jnp.full((1, BLOCK), MASKED, F32)
        for start, size in tiles:
            score = mm(k_s[start : start + size, :], query_t)
            if start >= base:
                seen = ids_col[start : start + size, :] <= ids_row[:, here]
                score = jnp.where(seen, score, MASKED)
            s_s[start : start + size, :] = score
            top = jnp.maximum(top, jnp.max(score, axis=0, keepdims=True))
        total = jnp.zeros((1, BLOCK), F32)
        att_t = jnp.zeros((HD, BLOCK), F32)
        for start, size in tiles:
            part = jnp.exp((s_s[start : start + size, :] - top) * SCALE)
            s_s[start : start + size, :] = part
            total = total + jnp.sum(part, axis=0, keepdims=True)
            low = part.astype(BF16)
            e_s[start : start + size, :] = low
            att_t = att_t + mm(v_t[:, start : start + size], low)
        inverse = 1.0 / total
        att_t = att_t * inverse
        att[here, :] = att_t.T.astype(BF16)
        grad_t = (g_t[:, here].astype(F32) * inverse).astype(BF16)
        grad_t_wide = grad_t.astype(F32)
        grad = grad_t_wide.T.astype(BF16)
        delta = jnp.sum(grad_t_wide * att_t, axis=0, keepdims=True)
        query = q_s[here, :]
        dq_t = jnp.zeros((HD, BLOCK), F32)
        for start, size in tiles:
            at = slice(start, start + size)
            dprob = mm(v_s[at, :], grad_t)
            dscore = (s_s[at, :] * (dprob - delta)).astype(BF16)
            dq_t = dq_t + mm(k_t[:, at], dscore)
            dk_s[at, :] += mm(dscore, query)
            dv_s[at, :] += mm(e_s[at, :], grad)
        grads[here, 0:HD] = (dq_t * SCALE).T.astype(BF16)
    grads[:, HD : 2 * HD] = (dk_s[...] * SCALE).astype(BF16)
    grads[:, 2 * HD : 3 * HD] = dv_s[...].astype(BF16)


def attention(core, packet_ids, own, other):
    low = pltpu.VMEM((TOK, HD), BF16)
    low_t = pltpu.VMEM((HD, TOK), BF16)
    vmem = pl.BlockSpec(memory_space=pltpu.VMEM)
    return pl.pallas_call(
        attention_kernel,
        out_shape=(
            jax.ShapeDtypeStruct((TOK, 3 * HD), BF16),
            jax.ShapeDtypeStruct((TOK, HD), BF16),
        ),
        in_specs=[pl.BlockSpec(memory_space=pltpu.SMEM), vmem, vmem, vmem, vmem],
        out_specs=(vmem, vmem),
        scratch_shapes=[low] * 4
        + [low_t] * 4
        + [
            pltpu.VMEM((TOK, BLOCK), F32),
            pltpu.VMEM((TOK, BLOCK), BF16),
            pltpu.VMEM((TOK, HD), F32),
            pltpu.VMEM((TOK, HD), F32),
        ],
        compiler_params=pltpu.CompilerParams(vmem_limit_bytes=48 * 1024 * 1024),
        name="attention",
    )(core[None], packet_ids[None, :], packet_ids[:, None], own, other)


def halves(core, own, other):
    return jnp.where(core == 0, own, other), jnp.where(core == 0, other, own)


def local(hidden_in, norm_gain, w_query, w_key, w_value, w_out, packet_ids, grad_out):
    row = lax.axis_index("row")
    col = lax.axis_index("col")
    core = row % 2
    odd = col % 2

    half = lax.dynamic_slice_in_dim(w_out, odd * 128, 128, 0)
    half_odd = lax.dynamic_slice_in_dim(w_out, (1 - odd) * 128, 128, 0)
    got = lax.ppermute(half, ("row", "col"), TURN)
    got_odd = lax.ppermute(half_odd, ("row", "col"), TURN_ODD)
    out_n = jnp.concatenate(halves(odd, got, got_odd), axis=1).T
    weights = jnp.concatenate([w_query, w_key, w_value, out_n], axis=1)
    w_own = spread(weights, "row", CHIPS)
    w_other = lax.ppermute(w_own, "row", CORE_SWAP)

    gain_rows = jnp.broadcast_to(norm_gain[None], (16, 128))
    pair = jnp.concatenate([hidden_in, grad_out, gain_rows], axis=0)
    far = lax.all_gather(pair, "col", axis=0, axis_index_groups=FAR)
    wide = spread(far.reshape(8, 272, 128), "col", NEAR).reshape(2, 2, 8, 272, 128)
    heads, both, recip = project(core, wide, w_own, w_other)
    heads_own = spread(heads, "row", CHIPS)

    both, heads_own = lax.optimization_barrier((both, heads_own))
    both = lax.all_to_all(both, "row", 0, 0, tiled=True)

    heads_other = lax.ppermute(heads_own, "row", CORE_SWAP)
    grads, attended = attention(core, packet_ids, heads_own, heads_other)

    parts = to_parts(core, row, grads, attended, wide, w_own, w_other)
    parts, both = lax.optimization_barrier((parts, both))
    tall = both.reshape(TOK, 512)
    grad_o = mm_tn(attended, tall[:, 256:])
    here, there = halves(odd, grad_o[:, :128], grad_o[:, 128:])
    parts, here, there = lax.optimization_barrier((parts, here, there))
    parts = lax.all_to_all(parts, "col", 0, 0, tiled=True, axis_index_groups=NEAR)
    parts = lax.all_to_all(merge(parts), "col", 0, 0, tiled=True, axis_index_groups=FAR)
    mixed, grad_x, gain_part = finish(parts, hidden_in, norm_gain, recip, grad_out)
    gain_all = lax.all_to_all(gain_part, "row", 0, 0, tiled=True)
    grad_gain = jnp.sum(gain_all, axis=(0, 1))

    grad_w = mm_tn(tall[:, :256], grads)
    got = lax.ppermute(here, ("row", "col"), TURN)
    got_odd = lax.ppermute(there, ("row", "col"), TURN_ODD)
    grad_w_out = jnp.concatenate(halves(odd, got, got_odd), axis=0)
    return (
        mixed,
        grad_x,
        grad_gain,
        grad_w[:, :128],
        grad_w[:, 128:256],
        grad_w[:, 256:],
        grad_w_out,
    )


def solution(mesh):
    tiled = P("row", "col")
    in_specs = (tiled, P("col"), tiled, tiled, tiled, tiled, P(), tiled)
    out_specs = (tiled, tiled, P("col"), tiled, tiled, tiled, tiled)
    return jax.shard_map(local, mesh=mesh, in_specs=in_specs, out_specs=out_specs, check_vma=False)
```

```python
import jax
import jax.numpy as jnp
from jax import lax
from jax.experimental import pallas as pl
from jax.experimental.pallas import tpu as pltpu
from jax.sharding import PartitionSpec as P

D = 4096
HD = 128
TOK = 2048
BLOCK = 256
OVER = 128
SCALE = HD ** (-0.5)
MASKED = -1e30
norm_eps = 1e-05

F32 = jnp.float32
BF16 = jnp.bfloat16


def col_at(a, h, l):
    return a * 16 + 2 * h + l


FAR = [[col_at(a, h, l) for h in range(8)] for a in range(2) for l in range(2)]
NEAR = [[col_at(a, h, l) for a in range(2) for l in range(2)] for h in range(8)]
CHIPS = [[2 * k + core for k in range(8)] for core in range(2)]
CORE_SWAP = [(r, r ^ 1) for r in range(16)]
TURN = [(r * 32 + c, (c // 2) * 32 + 2 * r + c % 2) for r in range(16) for c in range(32)]
COL_SWAP = [(c, c ^ 1) for c in range(32)]


def mm(a, b):
    return jnp.dot(a, b, preferred_element_type=F32)


def mm_nt(a, b):
    return lax.dot_general(a, b, (((1,), (1,)), ((), ())), preferred_element_type=F32)


def mm_tn(a, b):
    return lax.dot_general(a, b, (((0,), (0,)), ((), ())), preferred_element_type=F32)


def spread(x, axis, groups):
    n = len(groups[0])
    wide = jnp.broadcast_to(x[None], (n,) + x.shape)
    return lax.all_to_all(wide, axis, 0, 0, tiled=True, axis_index_groups=groups)


def flip(x):
    return x.astype(F32).T.astype(BF16)


def project_kernel(core_ref, wide, own, other, heads, both, recip_out):
    core = core_ref[0]
    squares = jnp.zeros((128, 128), F32)
    for a in range(2):
        for l in range(2):
            for h in range(8):
                x = wide[a, l, h, 0:128, :].astype(F32)
                squares = squares + x * x
    recip = lax.rsqrt(jnp.sum(squares, axis=1, keepdims=True) / D + norm_eps)
    recip_out[...] = recip
    qkv = jnp.zeros((128, 3 * HD), F32)
    grad = jnp.zeros((128, HD), F32)
    for k in range(8):
        for src, flag in ((own, core), (other, 1 - core)):
            h = 2 * (k % 4) + flag
            normed = []
            for l in range(2):
                x = wide[k // 4, l, h, 0:128, :].astype(F32)
                gain = wide[k // 4, l, h, 256:272, :].astype(F32)[0:1, :]
                normed.append((x * recip * gain).astype(BF16))
                go = wide[k // 4, l, h, 128:256, :]
                both[2 * k + flag, :, 256 + l * 128 : 384 + l * 128] = go
                grad = grad + mm_nt(go, src[k, 768 + l * 128 : 896 + l * 128, :])
            normed = jnp.concatenate(normed, axis=1)
            both[2 * k + flag, :, 0:256] = normed
            qkv = qkv + mm(normed, projections(src, k))
    heads[:, 0 : 3 * HD] = qkv.astype(BF16)
    heads[:, 3 * HD :] = grad.astype(BF16)


def projections(src, k):
    return jnp.concatenate([src[k, n * 256 : (n + 1) * 256, :] for n in range(3)], axis=1)


def project(core, wide, own, other):
    vmem = pl.BlockSpec(memory_space=pltpu.VMEM)
    return pl.pallas_call(
        project_kernel,
        out_shape=(
            jax.ShapeDtypeStruct((128, 4 * HD), BF16),
            jax.ShapeDtypeStruct((16, 128, 512), BF16),
            jax.ShapeDtypeStruct((128, 1), F32),
        ),
        in_specs=[pl.BlockSpec(memory_space=pltpu.SMEM), vmem, vmem, vmem],
        out_specs=(vmem, vmem, vmem),
        compiler_params=pltpu.CompilerParams(vmem_limit_bytes=48 * 1024 * 1024),
        name="project",
    )(core[None], wide, own, other)


def dot_rows(dot):
    high = dot.astype(BF16)
    low = (dot - high.astype(F32)).astype(BF16)
    at = lax.broadcasted_iota(jnp.int32, (16, 128), 0)
    wide = jnp.where(at == 0, high.astype(F32), jnp.where(at == 1, low.astype(F32), 0.0))
    return wide.astype(BF16)


def merge_kernel(parts, out):
    for h in range(8):
        total = parts[0, h].astype(F32)
        for n in range(1, 4):
            total = total + parts[n, h].astype(F32)
        out[h, 0:256, :] = total[0:256].astype(BF16)
        out[h, 256:272, :] = dot_rows(total[256:257] + total[257:258])


def merge(parts):
    vmem = pl.BlockSpec(memory_space=pltpu.VMEM)
    return pl.pallas_call(
        merge_kernel,
        out_shape=jax.ShapeDtypeStruct((8, 272, 128), BF16),
        in_specs=[vmem],
        out_specs=vmem,
        compiler_params=pltpu.CompilerParams(vmem_limit_bytes=48 * 1024 * 1024),
        name="merge",
    )(parts)


def finish_kernel(parts, hidden, gain_in, recip_in, grad_out, mixed, grad_x, gain_part):
    total = parts[0].astype(F32)
    for n in range(1, 8):
        total = total + parts[n].astype(F32)
    grad_normed = total[0:128]
    dot = total[256:257] + total[257:258]
    dot = jnp.broadcast_to(dot, (128, 128)).T
    x = hidden[...].astype(F32)
    recip = recip_in[...]
    mixed[...] = (x + total[128:256]).astype(BF16)
    scaled = grad_normed * gain_in[...].astype(F32)
    grad_x[...] = grad_out[...].astype(F32) + recip * scaled - x * (recip * recip * recip * dot / D)
    part = jnp.sum(grad_normed * x * recip, axis=0, keepdims=True)
    for n in range(16):
        gain_part[n] = part


def finish(parts, hidden, gain, recip, grad_out):
    vmem = pl.BlockSpec(memory_space=pltpu.VMEM)
    return pl.pallas_call(
        finish_kernel,
        out_shape=(
            jax.ShapeDtypeStruct((128, 128), BF16),
            jax.ShapeDtypeStruct((128, 128), F32),
            jax.ShapeDtypeStruct((16, 1, 128), F32),
        ),
        in_specs=[vmem] * 5,
        out_specs=(vmem, vmem, vmem),
        name="finish",
    )(parts, hidden, gain[None, :], recip, grad_out)


def attention_kernel(
    place, ids, own, other, wide_in, w_own_in, w_other_in, grads, att, parts,
    q_s, k_s, v_s, g_s, q_t, k_t, v_t, g_t, s_s, e_s, dk_s, dv_s,
    wide, w_own, w_other, sems,
):
    core, row = place[0], place[1]
    copies = [
        pltpu.make_async_copy(src, dst, sems.at[n])
        for n, (src, dst) in enumerate(
            ((wide_in, wide), (w_own_in, w_own), (w_other_in, w_other))
        )
    ]
    for copy in copies:
        copy.start()
    for k in range(8):
        for src, flag in ((own, core), (other, 1 - core)):
            at = pl.ds(pl.multiple_of((2 * k + flag) * 128, 128), 128)
            for n, (flat, turned) in enumerate(((q_s, q_t), (k_s, k_t), (v_s, v_t), (g_s, g_t))):
                piece = src[k, :, n * 128 : (n + 1) * 128]
                flat[at, :] = piece
                turned[:, at] = flip(piece)
    dk_s[...] = jnp.zeros_like(dk_s)
    dv_s[...] = jnp.zeros_like(dv_s)

    def tiles_of(i):
        tiles = [(j * BLOCK, BLOCK) for j in range(i + 1)]
        if (i + 1) * BLOCK < TOK:
            tiles.append(((i + 1) * BLOCK, OVER))
        return tiles

    def score_steps(i, state):
        base = i * BLOCK
        here = slice(base, base + BLOCK)
        top = jnp.full((1, BLOCK), MASKED, F32)
        for start, size in tiles_of(i):
            score = mm(k_s[start : start + size, :], q_t[:, here])
            if start >= base:
                ids_tile = jnp.broadcast_to(ids[:, start : start + size], (8, size))
                seen = ids_tile.T[:, 0:1] <= ids[:, here]
                score = jnp.where(seen, score, MASKED)
            s_s[i % 2, start : start + size, :] = score
            top = jnp.maximum(top, jnp.max(score, axis=0, keepdims=True))
            state["top"] = top
            yield

    def back_steps(i, state):
        base = i * BLOCK
        here = slice(base, base + BLOCK)
        top = state["top"]
        total = jnp.zeros((1, BLOCK), F32)
        att_t = jnp.zeros((HD, BLOCK), F32)
        for start, size in tiles_of(i):
            at = slice(start, start + size)
            part = jnp.exp((s_s[i % 2, at, :] - top) * SCALE)
            s_s[i % 2, at, :] = part
            total = total + jnp.sum(part, axis=0, keepdims=True)
            low = part.astype(BF16)
            e_s[i % 2, at, :] = low
            att_t = att_t + mm(v_t[:, at], low)
            yield
        inverse = 1.0 / total
        att_t = att_t * inverse
        att[here, :] = att_t.T.astype(BF16)
        grad_t = (g_t[:, here].astype(F32) * inverse).astype(BF16)
        grad_t_wide = grad_t.astype(F32)
        grad = grad_t_wide.T.astype(BF16)
        delta = jnp.sum(grad_t_wide * att_t, axis=0, keepdims=True)
        query = q_s[here, :]
        dq_t = jnp.zeros((HD, BLOCK), F32)
        for start, size in tiles_of(i):
            at = slice(start, start + size)
            dprob = mm(v_s[at, :], grad_t)
            dscore = (s_s[i % 2, at, :] * (dprob - delta)).astype(BF16)
            dq_t = dq_t + mm(k_t[:, at], dscore)
            dk_s[at, :] += mm(dscore, query)
            dv_s[at, :] += mm(e_s[i % 2, at, :], grad)
            yield
        grads[here, 0:HD] = (dq_t * SCALE).T.astype(BF16)

    blocks = TOK // BLOCK
    state = {}
    for _ in score_steps(0, state):
        pass
    for i in range(blocks):
        following = {}
        ahead = score_steps(i + 1, following) if i + 1 < blocks else iter(())
        for _ in back_steps(i, state):
            next(ahead, None)
        for _ in ahead:
            pass
        state = following
    grads[:, HD : 2 * HD] = (dk_s[...] * SCALE).astype(BF16)
    grads[:, 2 * HD : 3 * HD] = dv_s[...].astype(BF16)

    for copy in copies:
        copy.wait()
    here = pl.ds(pl.multiple_of(row * 128, 128), 128)
    grad, attended = grads[here, :], att[here, :]
    dots = jnp.zeros((128, 128), F32)
    for k in range(8):
        for src, flag in ((w_own, core), (w_other, 1 - core)):
            h = 2 * (k % 4) + flag
            back = mm_nt(grad, projections(src, k)).astype(BF16)
            for l in range(2):
                cut = back[:, l * 128 : (l + 1) * 128]
                x = wide[k // 4, l, h, 0:128, :].astype(F32)
                gain = wide[k // 4, l, h, 256:272, :].astype(F32)[0:1, :]
                dots = dots + cut.astype(F32) * gain * x
                parts[2 * (k // 4) + l, h, 0:128, :] = cut
                mixed = mm(attended, src[k, 768 + l * 128 : 896 + l * 128, :])
                parts[2 * (k // 4) + l, h, 128:256, :] = mixed.astype(BF16)
    extra = dot_rows(jnp.sum(dots.T, axis=0, keepdims=True))
    for n in range(4):
        for h in range(8):
            parts[n, h, 256:272, :] = extra


def attention(place, packet_ids, own, other, wide, w_own, w_other):
    low = pltpu.VMEM((TOK, HD), BF16)
    low_t = pltpu.VMEM((HD, TOK), BF16)
    vmem = pl.BlockSpec(memory_space=pltpu.VMEM)
    anywhere = pl.BlockSpec(memory_space=pl.ANY)
    return pl.pallas_call(
        attention_kernel,
        out_shape=(
            jax.ShapeDtypeStruct((TOK, 3 * HD), BF16),
            jax.ShapeDtypeStruct((TOK, HD), BF16),
            jax.ShapeDtypeStruct((4, 8, 272, 128), BF16),
        ),
        in_specs=[pl.BlockSpec(memory_space=pltpu.SMEM)] + [vmem] * 3 + [anywhere] * 3,
        out_specs=(vmem, vmem, vmem),
        scratch_shapes=[low] * 4
        + [low_t] * 4
        + [
            pltpu.VMEM((2, TOK, BLOCK), F32),
            pltpu.VMEM((2, TOK, BLOCK), BF16),
            pltpu.VMEM((TOK, HD), F32),
            pltpu.VMEM((TOK, HD), F32),
            pltpu.VMEM(wide.shape, BF16),
            pltpu.VMEM(w_own.shape, BF16),
            pltpu.VMEM(w_other.shape, BF16),
            pltpu.SemaphoreType.DMA((3,)),
        ],
        compiler_params=pltpu.CompilerParams(vmem_limit_bytes=56 * 1024 * 1024),
        name="attention",
    )(place, packet_ids.astype(F32)[None, :], own, other, wide, w_own, w_other)


def halves(core, own, other):
    return jnp.where(core == 0, own, other), jnp.where(core == 0, other, own)


def local(hidden_in, norm_gain, w_query, w_key, w_value, w_out, packet_ids, grad_out):
    row = lax.axis_index("row")
    col = lax.axis_index("col")
    core = row % 2
    odd = col % 2

    kept = lax.dynamic_slice_in_dim(w_out, odd * 128, 128, 0)
    got = lax.dynamic_slice_in_dim(w_out, (1 - odd) * 128, 128, 0)
    got = lax.ppermute(got, "col", COL_SWAP)
    out_n = jnp.concatenate(halves(odd, kept, got), axis=0)
    out_n = lax.ppermute(out_n, ("row", "col"), TURN)
    weights = jnp.concatenate([w_query, w_key, w_value, out_n], axis=0)
    w_own = spread(weights, "row", CHIPS)
    w_other = lax.ppermute(w_own, "row", CORE_SWAP)

    gain_rows = jnp.broadcast_to(norm_gain[None], (16, 128))
    pair = jnp.concatenate([hidden_in, grad_out, gain_rows], axis=0)
    far = lax.all_gather(pair, "col", axis=0, axis_index_groups=FAR)
    wide = spread(far.reshape(8, 272, 128), "col", NEAR).reshape(2, 2, 8, 272, 128)
    heads, both, recip = project(core, wide, w_own, w_other)
    heads_own = spread(heads, "row", CHIPS)

    both, heads_own = lax.optimization_barrier((both, heads_own))
    both = lax.all_to_all(both, "row", 0, 0, tiled=True)

    heads_other = lax.ppermute(heads_own, "row", CORE_SWAP)
    grads, attended, parts = attention(
        jnp.stack([core, row]), packet_ids, heads_own, heads_other, wide, w_own, w_other
    )
    parts, both = lax.optimization_barrier((parts, both))
    parts = lax.all_to_all(parts, "col", 0, 0, tiled=True, axis_index_groups=NEAR)
    parts = lax.all_to_all(merge(parts), "col", 0, 0, tiled=True, axis_index_groups=FAR)
    tall = both.reshape(TOK, 512)
    grad_w = mm_tn(tall[:, :256], grads)
    grad_o = mm_tn(tall[:, 256:], attended).astype(BF16)
    parts, grad_w, grad_o = lax.optimization_barrier((parts, grad_w, grad_o))

    mixed, grad_x, gain_part = finish(parts, hidden_in, norm_gain, recip, grad_out)
    gain_all = lax.all_to_all(gain_part, "row", 0, 0, tiled=True)
    grad_gain = jnp.sum(gain_all, axis=(0, 1))

    grad_o = lax.ppermute(grad_o, ("row", "col"), TURN)
    kept = lax.dynamic_slice_in_dim(grad_o, odd * 128, 128, 0)
    got = lax.dynamic_slice_in_dim(grad_o, (1 - odd) * 128, 128, 0)
    got = lax.ppermute(got, "col", COL_SWAP)
    grad_w_out = jnp.concatenate(halves(odd, kept.T, got.T), axis=0).astype(F32)
    return (
        mixed,
        grad_x,
        grad_gain,
        grad_w[:, :128],
        grad_w[:, 128:256],
        grad_w[:, 256:],
        grad_w_out,
    )


def solution(mesh):
    tiled = P("row", "col")
    in_specs = (tiled, P("col"), tiled, tiled, tiled, tiled, P(), tiled)
    out_specs = (tiled, tiled, P("col"), tiled, tiled, tiled, tiled)
    return jax.shard_map(local, mesh=mesh, in_specs=in_specs, out_specs=out_specs, check_vma=False)
```

```python
import jax
import jax.numpy as jnp
from jax import lax
from jax.experimental import pallas as pl
from jax.experimental.pallas import tpu as pltpu
from jax.sharding import PartitionSpec as P

D = 4096
HD = 128
TOK = 2048
BLOCK = 512
OVER = 128
SCALE = HD ** (-0.5)
MASKED = -1e30
norm_eps = 1e-05

F32 = jnp.float32
BF16 = jnp.bfloat16


def col_at(a, h, l):
    return a * 16 + 2 * h + l


FAR = [[col_at(a, h, l) for h in range(8)] for a in range(2) for l in range(2)]
NEAR = [[col_at(a, h, l) for a in range(2) for l in range(2)] for h in range(8)]
CHIPS = [[2 * k + core for k in range(8)] for core in range(2)]
CORE_SWAP = [(r, r ^ 1) for r in range(16)]
TURN = [(r * 32 + c, (c // 2) * 32 + 2 * r + c % 2) for r in range(16) for c in range(32)]
COL_SWAP = [(c, c ^ 1) for c in range(32)]


def mm(a, b):
    return jnp.dot(a, b, preferred_element_type=F32)


def mm_nt(a, b):
    return lax.dot_general(a, b, (((1,), (1,)), ((), ())), preferred_element_type=F32)


def mm_tn(a, b):
    return lax.dot_general(a, b, (((0,), (0,)), ((), ())), preferred_element_type=F32)


def spread(x, axis, groups):
    n = len(groups[0])
    wide = jnp.broadcast_to(x[None], (n,) + x.shape)
    return lax.all_to_all(wide, axis, 0, 0, tiled=True, axis_index_groups=groups)


def flip(x):
    return x.astype(F32).T.astype(BF16)


def project_kernel(
    core_ref, wide, own_in, other_in, heads, both, recip_out, own, other, sems
):
    copies = [
        pltpu.make_async_copy(own_in, own, sems.at[0]),
        pltpu.make_async_copy(other_in, other, sems.at[1]),
    ]
    for copy in copies:
        copy.start()
    core = core_ref[0]
    squares = jnp.zeros((128, 128), F32)
    for a in range(2):
        for l in range(2):
            for h in range(8):
                x = wide[a, l, h, 0:128, :].astype(F32)
                squares = squares + x * x
    recip = lax.rsqrt(jnp.sum(squares, axis=1, keepdims=True) / D + norm_eps)
    recip_out[...] = recip
    for copy in copies:
        copy.wait()
    qkv = jnp.zeros((128, 3 * HD), F32)
    grad = jnp.zeros((128, HD), F32)
    for k in range(8):
        for src, flag in ((own, core), (other, 1 - core)):
            h = 2 * (k % 4) + flag
            normed = []
            for l in range(2):
                x = wide[k // 4, l, h, 0:128, :].astype(F32)
                gain = wide[k // 4, l, h, 256:272, :].astype(F32)[0:1, :]
                normed.append((x * recip * gain).astype(BF16))
                go = wide[k // 4, l, h, 128:256, :]
                both[2 * k + flag, :, 256 + l * 128 : 384 + l * 128] = go
                grad = grad + mm_nt(go, src[k, 768 + l * 128 : 896 + l * 128, :])
            normed = jnp.concatenate(normed, axis=1)
            both[2 * k + flag, :, 0:256] = normed
            qkv = qkv + mm(normed, projections(src, k))
    heads[:, 0 : 3 * HD] = qkv.astype(BF16)
    heads[:, 3 * HD :] = grad.astype(BF16)


def projections(src, k):
    return jnp.concatenate([src[k, n * 256 : (n + 1) * 256, :] for n in range(3)], axis=1)


def project(core, wide, own, other):
    vmem = pl.BlockSpec(memory_space=pltpu.VMEM)
    return pl.pallas_call(
        project_kernel,
        out_shape=(
            jax.ShapeDtypeStruct((128, 4 * HD), BF16),
            jax.ShapeDtypeStruct((16, 128, 512), BF16),
            jax.ShapeDtypeStruct((128, 1), F32),
        ),
        in_specs=[pl.BlockSpec(memory_space=pltpu.SMEM), vmem]
        + [pl.BlockSpec(memory_space=pl.ANY)] * 2,
        out_specs=(vmem, vmem, vmem),
        scratch_shapes=[
            pltpu.VMEM(own.shape, BF16),
            pltpu.VMEM(other.shape, BF16),
            pltpu.SemaphoreType.DMA((2,)),
        ],
        compiler_params=pltpu.CompilerParams(vmem_limit_bytes=48 * 1024 * 1024),
        name="project",
    )(core[None], wide, own, other)


def dot_rows(dot):
    high = dot.astype(BF16)
    low = (dot - high.astype(F32)).astype(BF16)
    at = lax.broadcasted_iota(jnp.int32, (16, 128), 0)
    wide = jnp.where(at == 0, high.astype(F32), jnp.where(at == 1, low.astype(F32), 0.0))
    return wide.astype(BF16)


def merge_kernel(parts, out):
    for h in range(8):
        total = parts[0, h].astype(F32)
        for n in range(1, 4):
            total = total + parts[n, h].astype(F32)
        out[h, 0:256, :] = total[0:256].astype(BF16)
        out[h, 256:272, :] = dot_rows(total[256:257] + total[257:258])


def merge(parts):
    vmem = pl.BlockSpec(memory_space=pltpu.VMEM)
    return pl.pallas_call(
        merge_kernel,
        out_shape=jax.ShapeDtypeStruct((8, 272, 128), BF16),
        in_specs=[vmem],
        out_specs=vmem,
        compiler_params=pltpu.CompilerParams(vmem_limit_bytes=48 * 1024 * 1024),
        name="merge",
    )(parts)


def finish_kernel(parts, hidden, gain_in, recip_in, grad_out, mixed, grad_x, gain_part):
    total = parts[0].astype(F32)
    for n in range(1, 8):
        total = total + parts[n].astype(F32)
    grad_normed = total[0:128]
    dot = total[256:257] + total[257:258]
    dot = jnp.broadcast_to(dot, (128, 128)).T
    x = hidden[...].astype(F32)
    recip = recip_in[...]
    mixed[...] = (x + total[128:256]).astype(BF16)
    scaled = grad_normed * gain_in[...].astype(F32)
    grad_x[...] = grad_out[...].astype(F32) + recip * scaled - x * (recip * recip * recip * dot / D)
    part = jnp.sum(grad_normed * x * recip, axis=0, keepdims=True)
    for n in range(16):
        gain_part[n] = part


def finish(parts, hidden, gain, recip, grad_out):
    vmem = pl.BlockSpec(memory_space=pltpu.VMEM)
    return pl.pallas_call(
        finish_kernel,
        out_shape=(
            jax.ShapeDtypeStruct((128, 128), BF16),
            jax.ShapeDtypeStruct((128, 128), F32),
            jax.ShapeDtypeStruct((16, 1, 128), F32),
        ),
        in_specs=[vmem] * 5,
        out_specs=(vmem, vmem, vmem),
        name="finish",
    )(parts, hidden, gain[None, :], recip, grad_out)


def attention_kernel(
    place, ids, own, other, wide_in, w_own_in, w_other_in, grads, att, parts,
    q_s, k_s, v_s, k_t, v_t, g_t, s_s, e_s, dk_s, dv_s,
    wide, w_own, w_other, sems,
):
    core, row = place[0], place[1]
    copies = [
        pltpu.make_async_copy(src, dst, sems.at[n])
        for n, (src, dst) in enumerate(
            ((wide_in, wide), (w_own_in, w_own), (w_other_in, w_other))
        )
    ]
    for copy in copies:
        copy.start()
    for k in range(8):
        for src, flag in ((own, core), (other, 1 - core)):
            at = pl.ds(pl.multiple_of((2 * k + flag) * 128, 128), 128)
            query, key, value, grad = [src[k, :, n * 128 : (n + 1) * 128] for n in range(4)]
            q_s[at, :] = query
            k_s[at, :] = key
            v_s[at, :] = value
            k_t[:, at] = flip(key)
            v_t[:, at] = flip(value)
            g_t[:, at] = flip(grad)
    dk_s[...] = jnp.zeros_like(dk_s)
    dv_s[...] = jnp.zeros_like(dv_s)

    def tiles_of(i):
        tiles = [(j * BLOCK, BLOCK) for j in range(i + 1)]
        if (i + 1) * BLOCK < TOK:
            tiles.append(((i + 1) * BLOCK, OVER))
        return tiles

    def score_steps(i, state):
        base = i * BLOCK
        here = slice(base, base + BLOCK)
        top = jnp.full((1, BLOCK), MASKED, F32)
        for start, size in tiles_of(i):
            score = mm_nt(k_s[start : start + size, :], q_s[here, :])
            if start >= base:
                ids_tile = jnp.broadcast_to(ids[:, start : start + size], (8, size))
                seen = ids_tile.T[:, 0:1] <= ids[:, here]
                score = jnp.where(seen, score, MASKED)
            s_s[i % 2, start : start + size, :] = score
            top = jnp.maximum(top, jnp.max(score, axis=0, keepdims=True))
            state["top"] = top
            yield

    def back_steps(i, state):
        base = i * BLOCK
        here = slice(base, base + BLOCK)
        top = state["top"]
        total = jnp.zeros((1, BLOCK), F32)
        att_t = jnp.zeros((HD, BLOCK), F32)
        for start, size in tiles_of(i):
            at = slice(start, start + size)
            part = jnp.exp((s_s[i % 2, at, :] - top) * SCALE)
            total = total + jnp.sum(part, axis=0, keepdims=True)
            low = part.astype(BF16)
            e_s[i % 2, at, :] = low
            att_t = att_t + mm(v_t[:, at], low)
            yield
        inverse = 1.0 / total
        att_t = att_t * inverse
        att[here, :] = att_t.T.astype(BF16)
        grad_t = (g_t[:, here].astype(F32) * inverse).astype(BF16)
        grad_t_wide = grad_t.astype(F32)
        grad = grad_t_wide.T.astype(BF16)
        delta = jnp.sum(grad_t_wide * att_t, axis=0, keepdims=True)
        query = q_s[here, :]
        dq_t = jnp.zeros((HD, BLOCK), F32)
        for start, size in tiles_of(i):
            at = slice(start, start + size)
            dprob = mm(v_s[at, :], grad_t)
            dscore = (e_s[i % 2, at, :].astype(F32) * (dprob - delta)).astype(BF16)
            dq_t = dq_t + mm(k_t[:, at], dscore)
            dk_s[at, :] += mm(dscore, query)
            dv_s[at, :] += mm(e_s[i % 2, at, :], grad)
            yield
        grads[here, 0:HD] = (dq_t * SCALE).T.astype(BF16)

    blocks = TOK // BLOCK
    state = {}
    for _ in score_steps(0, state):
        pass
    for i in range(blocks):
        following = {}
        ahead = score_steps(i + 1, following) if i + 1 < blocks else iter(())
        for _ in back_steps(i, state):
            next(ahead, None)
        for _ in ahead:
            pass
        state = following
    grads[:, HD : 2 * HD] = (dk_s[...] * SCALE).astype(BF16)
    grads[:, 2 * HD : 3 * HD] = dv_s[...].astype(BF16)

    for copy in copies:
        copy.wait()
    here = pl.ds(pl.multiple_of(row * 128, 128), 128)
    grad, attended = grads[here, :], att[here, :]
    dots = jnp.zeros((128, 128), F32)
    for k in range(8):
        for src, flag in ((w_own, core), (w_other, 1 - core)):
            h = 2 * (k % 4) + flag
            back = mm_nt(grad, projections(src, k)).astype(BF16)
            for l in range(2):
                cut = back[:, l * 128 : (l + 1) * 128]
                x = wide[k // 4, l, h, 0:128, :].astype(F32)
                gain = wide[k // 4, l, h, 256:272, :].astype(F32)[0:1, :]
                dots = dots + cut.astype(F32) * gain * x
                parts[2 * (k // 4) + l, h, 0:128, :] = cut
                mixed = mm(attended, src[k, 768 + l * 128 : 896 + l * 128, :])
                parts[2 * (k // 4) + l, h, 128:256, :] = mixed.astype(BF16)
    extra = dot_rows(jnp.sum(dots.T, axis=0, keepdims=True))
    for n in range(4):
        for h in range(8):
            parts[n, h, 256:272, :] = extra


def attention(place, packet_ids, own, other, wide, w_own, w_other):
    low = pltpu.VMEM((TOK, HD), BF16)
    low_t = pltpu.VMEM((HD, TOK), BF16)
    vmem = pl.BlockSpec(memory_space=pltpu.VMEM)
    anywhere = pl.BlockSpec(memory_space=pl.ANY)
    return pl.pallas_call(
        attention_kernel,
        out_shape=(
            jax.ShapeDtypeStruct((TOK, 3 * HD), BF16),
            jax.ShapeDtypeStruct((TOK, HD), BF16),
            jax.ShapeDtypeStruct((4, 8, 272, 128), BF16),
        ),
        in_specs=[pl.BlockSpec(memory_space=pltpu.SMEM)] + [vmem] * 3 + [anywhere] * 3,
        out_specs=(vmem, vmem, vmem),
        scratch_shapes=[low] * 3
        + [low_t] * 3
        + [
            pltpu.VMEM((2, TOK, BLOCK), F32),
            pltpu.VMEM((2, TOK, BLOCK), BF16),
            pltpu.VMEM((TOK, HD), F32),
            pltpu.VMEM((TOK, HD), F32),
            pltpu.VMEM(wide.shape, BF16),
            pltpu.VMEM(w_own.shape, BF16),
            pltpu.VMEM(w_other.shape, BF16),
            pltpu.SemaphoreType.DMA((3,)),
        ],
        compiler_params=pltpu.CompilerParams(vmem_limit_bytes=56 * 1024 * 1024),
        name="attention",
    )(place, packet_ids.astype(F32)[None, :], own, other, wide, w_own, w_other)


def halves(core, own, other):
    return jnp.where(core == 0, own, other), jnp.where(core == 0, other, own)


def local(hidden_in, norm_gain, w_query, w_key, w_value, w_out, packet_ids, grad_out):
    row = lax.axis_index("row")
    col = lax.axis_index("col")
    core = row % 2
    odd = col % 2

    kept = lax.dynamic_slice_in_dim(w_out, odd * 128, 128, 0)
    got = lax.dynamic_slice_in_dim(w_out, (1 - odd) * 128, 128, 0)
    got = lax.ppermute(got, "col", COL_SWAP)
    out_n = jnp.concatenate(halves(odd, kept, got), axis=0)
    out_n = lax.ppermute(out_n, ("row", "col"), TURN)
    weights = jnp.concatenate([w_query, w_key, w_value, out_n], axis=0)
    w_own = spread(weights, "row", CHIPS)
    w_other = lax.ppermute(w_own, "row", CORE_SWAP)

    gain_rows = jnp.broadcast_to(norm_gain[None], (16, 128))
    pair = jnp.concatenate([hidden_in, grad_out, gain_rows], axis=0)
    far = lax.all_gather(pair, "col", axis=0, axis_index_groups=FAR)
    wide = spread(far.reshape(8, 272, 128), "col", NEAR).reshape(2, 2, 8, 272, 128)
    heads, both, recip = project(core, wide, w_own, w_other)
    heads_own = spread(heads, "row", CHIPS)

    both, heads_own = lax.optimization_barrier((both, heads_own))
    both = lax.all_to_all(both, "row", 0, 0, tiled=True)

    heads_other = lax.ppermute(heads_own, "row", CORE_SWAP)
    grads, attended, parts = attention(
        jnp.stack([core, row]), packet_ids, heads_own, heads_other, wide, w_own, w_other
    )
    parts, both = lax.optimization_barrier((parts, both))
    parts = lax.all_to_all(parts, "col", 0, 0, tiled=True, axis_index_groups=NEAR)
    parts = lax.all_to_all(merge(parts), "col", 0, 0, tiled=True, axis_index_groups=FAR)
    tall = both.reshape(TOK, 512)
    grad_w = mm_tn(tall[:, :256], grads)
    grad_o = mm_tn(tall[:, 256:], attended).astype(BF16)
    parts, grad_w, grad_o = lax.optimization_barrier((parts, grad_w, grad_o))

    mixed, grad_x, gain_part = finish(parts, hidden_in, norm_gain, recip, grad_out)
    gain_part, grad_o = lax.optimization_barrier((gain_part, grad_o))
    gain_all = lax.all_to_all(gain_part, "row", 0, 0, tiled=True)
    grad_gain = jnp.sum(gain_all, axis=(0, 1))

    grad_o = lax.ppermute(grad_o, ("row", "col"), TURN)
    kept = lax.dynamic_slice_in_dim(grad_o, odd * 128, 128, 0)
    got = lax.dynamic_slice_in_dim(grad_o, (1 - odd) * 128, 128, 0)
    got = lax.ppermute(got, "col", COL_SWAP)
    grad_w_out = jnp.concatenate(halves(odd, kept.T, got.T), axis=0).astype(F32)
    return (
        mixed,
        grad_x,
        grad_gain,
        grad_w[:, :128],
        grad_w[:, 128:256],
        grad_w[:, 256:],
        grad_w_out,
    )


def solution(mesh):
    tiled = P("row", "col")
    in_specs = (tiled, P("col"), tiled, tiled, tiled, tiled, P(), tiled)
    out_specs = (tiled, tiled, P("col"), tiled, tiled, tiled, tiled)
    return jax.shard_map(local, mesh=mesh, in_specs=in_specs, out_specs=out_specs, check_vma=False)
```
